128 devices in a mesh: replica: 8 (over x_hi, z), section: 16 (over y, x_lo, core).
Axes of the slice: x: 4 (x_hi: 2, x_lo: 2; x = x_hi * 2 + x_lo), y: 4, z: 4, core: 2. Of those that a mesh axis runs over, the one named last changes fastest.
Arguments:
- gradients: bfloat16 [8, 256, 512, 128], P('replica', 'section'), may hold values from -6 to 6
- master: float32 [256, 512, 128], P('section', 'replica'), may hold values from -0.25 to 0.25
- moment_one: float32 [256, 512, 128], P('section', 'replica'), may hold values from -4 to 4
- moment_two: float32 [256, 512, 128], P('section', 'replica'), may hold values from 0.01 to 4
- new_owner: int32 [256, 1], replicated, may hold values from 0 to 14; in each aligned block of 16 rows (0 to 15, 16 to 31, ...) at most 2 rows name the same one
Outputs:
- new_master: float32 [16, 16, 2, 512, 128], P('section', None, None, 'replica')
- new_moment_one: float32 [16, 16, 2, 512, 128], P('section', None, None, 'replica')
- new_moment_two: float32 [16, 16, 2, 512, 128], P('section', None, None, 'replica')
- new_weights: bfloat16 [16, 16, 2, 512, 128], P('section')
The draws below stay inside these ranges and needn't reach their ends.
Inputs may be any that keep to these rules, and one draw needn't show every extreme that they name: `new_owner`: among the 16 blocks of one old section, no new section is named more than 2 times. No block goes to section 15.
All inputs are finite; a program needn't handle non-finite values.
Results may differ from the reference program's by a relative error of at most 0.01.
Values may be sent and summed in bfloat16 or wider, within the bound.
A program may use at most 64 MiB of HBM per device.

```python
import math
import jax
import jax.numpy as jnp
import numpy as np
from jax import lax

LANES = 128
PAIR = 2
ROWS = 512
SECTION_BLOCKS = 16
BLOCKS = 256
N_REPLICA = 8
N_SECTION = 16


def levels(rng, extent, split, low, high):
    loudness = 1.0
    for dim, blocks in split:
        heights = jax.random.uniform(jax.random.fold_in(jax.random.fold_in(rng, 6), dim), (blocks,), jnp.float32, low / len(split), high / len(split))
        loudness = loudness * jnp.repeat(jnp.exp(heights), extent[dim] // blocks).reshape((-1,) + (1,) * (len(extent) - 1 - dim))
    return loudness


def shared_out(key, own, number, rows, number_of, top, reach, lean):
    sequence = jax.random.permutation(key, number_of)
    crowded, usual = shares(number_of, rows * top, reach, lean, True), shares(number_of, rows * top, reach, lean, False)
    places = jnp.arange(number_of)

    def named(sizes, turn):
        used = int((sizes > 0).sum())
        fixed = max(1, used // 4)
        moved = fixed + (places - fixed + turn * (used - fixed)) % max(1, number_of - fixed)
        return jnp.zeros((number_of,), jnp.int32).at[sequence[jnp.where(places < fixed, places, moved)]].set(jnp.asarray(sizes, jnp.int32))

    sizes = jnp.where(number % 4 == 0, named(crowded, number // 4), named(usual, number - number // 4 - 1))
    mixed = jax.random.permutation(jax.random.fold_in(own, 3), number_of)
    source_of, taker = mixed[0:number_of // 2 * 2:2], mixed[1:number_of // 2 * 2:2]
    margin = jnp.minimum(sizes[source_of] - 1, reach - sizes[taker]) // 2
    margin = jnp.where((source_of == sequence[0]) | (taker == sequence[0]) | (sizes[taker] == 0), 0, jnp.maximum(margin, 0))
    moved = jax.random.randint(jax.random.fold_in(own, 4), (number_of // 2,), 0, 1 << 20) % (margin + 1)
    sizes = sizes.at[source_of].add(-moved).at[taker].add(moved)
    items = jnp.searchsorted(jnp.cumsum(sizes), jnp.arange(rows * top), side="right").astype(jnp.int32)
    table = items.reshape(top, rows).T
    table = table[jax.random.permutation(jax.random.fold_in(own, 1), rows)]
    turn = jax.random.randint(jax.random.fold_in(own, 2), (rows, 1), 0, top)
    return jnp.take_along_axis(table, (jnp.arange(top)[None, :] + turn) % top, axis=1)


def shares(number_of, total, reach, lean, full):
    weights = [(1 << 20) // math.isqrt(standing ** lean) + 1 for standing in range(1, number_of + 1)]
    largest = reach if full else min(reach, max(-(-total // number_of), total * weights[0] // sum(weights)))
    least = 1 if total - largest >= number_of - 1 else 0
    holding, spare = [largest] + [least] * (number_of - 1), total - largest - least * (number_of - 1)
    while spare > 0:
        free = [i for i in range(1, number_of) if holding[i] < largest] or [i for i in range(1, number_of) if holding[i] < reach]
        mass, remaining = sum([weights[i] for i in free]), spare
        for i in free:
            extra = min(reach - holding[i], max(1, remaining * weights[i] // mass), spare)
            holding[i] = holding[i] + extra
            spare = spare - extra
    return np.array(holding)


def noise(stream_key, extent, width, limit, cuts=(), held_as=jnp.bfloat16):
    factor_of = levels(stream_key, extent, cuts, -0.22, 0.18) if cuts else 1.0
    result = jax.random.normal(stream_key, extent, jnp.float32) * width * factor_of
    return jnp.minimum(jnp.maximum(result, -limit), limit).astype(held_as)


def setup_inputs(seed: int = 0) -> dict:
    key_of = jax.random.split(jax.random.key(seed), 6)
    gradients = noise(key_of[0], (N_REPLICA, BLOCKS, ROWS, LANES), 1.0, 6.0, ((0, 8), (1, 16)))
    master = noise(key_of[1], (BLOCKS, ROWS, LANES), 0.1, 0.25, ((0, 16), (1, 8)), jnp.float32)
    moment_one = noise(key_of[2], (BLOCKS, ROWS, LANES), 0.5, 4.0, ((0, 16), (1, 8)), jnp.float32)
    moment_two = jnp.clip(jnp.exp(math.log(4.0) - 5.9914646 * jax.random.uniform(key_of[3], (BLOCKS, ROWS, LANES), jnp.float32) ** levels(key_of[3], (BLOCKS, ROWS, LANES), ((0, 16), (1, 8)), -0.2, 0.2)), 0.01, 4.0)
    new_owner_keys = jax.random.split(jax.random.fold_in(key_of[4], 1), BLOCKS // SECTION_BLOCKS)
    new_owner_turns = jax.random.permutation(jax.random.fold_in(key_of[4], 3), BLOCKS // SECTION_BLOCKS)
    new_owner = jax.vmap(lambda own, number: shared_out(jax.random.fold_in(key_of[4], 2), own, number, SECTION_BLOCKS, N_SECTION - 1, 1, PAIR, 2))(new_owner_keys, new_owner_turns).reshape((BLOCKS, 1))
    return dict(gradients=gradients, master=master, moment_one=moment_one, moment_two=moment_two, new_owner=new_owner)


beta_one = 0.9
beta_two = 0.95
step_count = 10.0
learn_rate = 0.01
decay_rate = 0.1
epsilon = 1e-08
correct_one = 1.0 - beta_one ** step_count
correct_two = 1.0 - beta_two ** step_count

def adamw_update(master, moment_one, moment_two, gradient):
    upd_one = beta_one * moment_one + (1.0 - beta_one) * gradient
    upd_two = beta_two * moment_two + (1.0 - beta_two) * gradient * gradient
    direction = upd_one / correct_one / (jnp.sqrt(upd_two / correct_two) + epsilon)
    upd_master = master - learn_rate * (direction + decay_rate * master)
    return (upd_master, upd_one, upd_two)

def reference(gradients, master, moment_one, moment_two, new_owner):
    summed = jnp.zeros(master.shape, jnp.float32)
    for replica_index in range(N_REPLICA):
        summed = summed + gradients[replica_index].astype(jnp.float32)
    upd_master, upd_one, upd_two = adamw_update(master, moment_one, moment_two, summed)
    owners = new_owner[:, 0].astype(jnp.int32)
    total_blocks = owners.shape[0]
    per_section = total_blocks // N_SECTION
    indices = jnp.arange(total_blocks, dtype=jnp.int32)
    source_section = (indices // per_section).astype(jnp.int32)
    matches = (owners[:, None] == owners[None, :]) & (source_section[:, None] == source_section[None, :]) & (indices[None, :] < indices[:, None])
    position = lax.optimization_barrier(jnp.sum(matches.astype(jnp.int32), axis=1)).astype(jnp.int32)

    def place(values):
        empty = jnp.zeros((N_SECTION, N_SECTION, PAIR) + values.shape[1:], values.dtype)
        return empty.at[owners, source_section, position].set(values)
    new_master = place(upd_master)
    return (new_master, place(upd_one), place(upd_two), new_master.astype(jnp.bfloat16))
```

```python
import functools

import jax
import jax.numpy as jnp
from jax import lax
from jax.experimental import pallas as pl
from jax.experimental.pallas import tpu as pltpu
from jax.sharding import PartitionSpec as P

MESH = pl.DeviceIdType.MESH
PAIR = 2
PARTS = 2

beta_one = 0.9
beta_two = 0.95
step_count = 10.0
learn_rate = 0.01
decay_rate = 0.1
epsilon = 1e-08
correct_one = 1.0 - beta_one**step_count
correct_two = 1.0 - beta_two**step_count


def adamw_update(master, moment_one, moment_two, gradient):
    upd_one = beta_one * moment_one + (1.0 - beta_one) * gradient
    upd_two = beta_two * moment_two + (1.0 - beta_two) * gradient * gradient
    direction = upd_one / correct_one / (jnp.sqrt(upd_two / correct_two) + epsilon)
    upd_master = master - learn_rate * (direction + decay_rate * master)
    return (upd_master, upd_one, upd_two)


def kernel(
    sections,
    owner_ref,
    grads_ref,
    master_ref,
    one_ref,
    two_ref,
    out_master,
    out_one,
    out_two,
    weights,
    own,
    mid_own,
    mid_in,
    mid_out,
    near,
    half_out,
    half_in,
    upd,
    sendbuf,
    moments,
    chosen,
    filled,
    load_sem,
    step_send,
    step_recv,
    mid_send,
    mid_recv,
    half_send,
    half_recv,
    mom_send,
    mom_recv,
    own_send,
    own_recv,
    far_send,
    far_recv,
    ring_send,
    ring_recv,
    fwd_send,
    fwd_recv,
):
    blocks = master_ref.shape[0]
    rows = master_ref.shape[1]
    part_rows = rows // PARTS
    r = lax.axis_index("replica")
    s = lax.axis_index("section")
    xh = r // 4
    z = r % 4
    up = lax.rem(z + 1, 4)
    down = lax.rem(z + 3, 4)
    opposite = lax.rem(z + 2, 4)
    dev_up = (xh * 4 + up, s)
    dev_down = (xh * 4 + down, s)
    partner = (1 - xh) * 4 + z

    def part(c):
        return pl.ds(c * part_rows, part_rows)

    def remote(src, dst, send, recv, device):
        return pltpu.make_async_remote_copy(
            src_ref=src, dst_ref=dst, send_sem=send, recv_sem=recv,
            device_id=device, device_id_type=MESH,
        )

    loads = []
    for c in range(PARTS):
        for k, (src, dst) in enumerate((
            (grads_ref.at[:, 0, up, part(c)], mid_own.at[0, :, part(c)]),
            (grads_ref.at[:, 1, down, part(c)], mid_own.at[1, :, part(c)]),
            (grads_ref.at[:, :, z, part(c)], own.at[:, :, part(c)]),
        )):
            copy = pltpu.make_async_copy(src, dst, load_sem.at[c, k])
            copy.start()
            loads.append(copy)

    barrier = pltpu.get_barrier_semaphore()
    pl.semaphore_signal(barrier, inc=1, device_id=dev_up, device_id_type=MESH)
    pl.semaphore_signal(barrier, inc=1, device_id=dev_down, device_id_type=MESH)
    pl.semaphore_signal(barrier, inc=1, device_id=(partner, s), device_id_type=MESH)

    def greet(i, _):
        t = lax.rem(s + i, sections)
        pl.semaphore_signal(barrier, inc=1, device_id=(r, t), device_id_type=MESH)
        pl.semaphore_signal(barrier, inc=1, device_id=(partner, t), device_id_type=MESH)
        return 0

    lax.fori_loop(1, sections, greet, 0)
    pl.semaphore_wait(barrier, 3 + 2 * (sections - 1))

    first = []
    for c in range(PARTS):
        rc = part(c)
        first.append((
            remote(grads_ref.at[:, 0, opposite, rc], mid_in.at[0, :, rc], step_send.at[c, 0], step_recv.at[c, 0], dev_up),
            remote(grads_ref.at[:, 1, opposite, rc], mid_in.at[1, :, rc], step_send.at[c, 1], step_recv.at[c, 1], dev_down),
            remote(grads_ref.at[:, 1, up, rc], near.at[0, 1, :, rc], step_send.at[c, 2], step_recv.at[c, 2], dev_up),
            remote(grads_ref.at[:, 0, down, rc], near.at[1, 0, :, rc], step_send.at[c, 3], step_recv.at[c, 3], dev_down),
        ))
        for copy in first[c]:
            copy.start()

    for t in range(sections):
        one_at = jnp.int32(0)
        last_at = jnp.int32(0)
        count = jnp.int32(0)
        for i in reversed(range(blocks)):
            same = owner_ref[0, s * blocks + i] == t
            one_at = jnp.where(same, i, one_at)
            last_at = jnp.where(same & (count == 0), i, last_at)
            count = count + jnp.where(same, 1, 0)
        chosen[t * PAIR] = one_at
        chosen[t * PAIR + 1] = last_at
        filled[t * PAIR] = jnp.where(count > 0, 1, 0)
        filled[t * PAIR + 1] = jnp.where(count > 1, 1, 0)

    second = [None] * PARTS

    def join(c):
        rc = part(c)
        second[c] = (
            remote(mid_out.at[0, :, rc], near.at[0, 0, :, rc], mid_send.at[c, 0], mid_recv.at[c, 0], dev_up),
            remote(mid_out.at[1, :, rc], near.at[1, 1, :, rc], mid_send.at[c, 1], mid_recv.at[c, 1], dev_down),
        )
        for h in range(2):
            loads[3 * c + h].wait()
            first[c][h].wait_recv()

            def add(b, _, h=h):
                mid_out[h, b, rc] = (
                    mid_in[h, b, rc].astype(jnp.float32) + mid_own[h, b, rc].astype(jnp.float32)
                ).astype(jnp.bfloat16)
                return 0

            lax.fori_loop(0, blocks, add, 0)
            second[c][h].start()

    def z_sum(c, b, h):
        rc = part(c)
        return (
            own[b, h, rc].astype(jnp.float32)
            + near[0, h, b, rc].astype(jnp.float32)
            + near[1, h, b, rc].astype(jnp.float32)
        )

    third = [None] * PARTS

    def cross(c):
        rc = part(c)
        loads[3 * c + 2].wait()
        first[c][2].wait_recv()
        first[c][3].wait_recv()
        second[c][0].wait_recv()
        second[c][1].wait_recv()

        def add(b, _):
            half_out[b, rc] = z_sum(c, b, 1 - xh).astype(jnp.bfloat16)
            return 0

        lax.fori_loop(0, blocks, add, 0)
        third[c] = remote(half_out.at[:, rc], half_in.at[:, rc], half_send.at[c], half_recv.at[c], (partner, s))
        third[c].start()

    def mom_copy(c, t):
        return remote(
            sendbuf.at[t, pl.ds(1, 2), :, part(c)], moments.at[s, :, :, part(c)],
            mom_send.at[c, t], mom_recv.at[c, s], (r, t),
        )

    def own_copy(c, t):
        return remote(
            sendbuf.at[t, 0, :, part(c)], weights.at[s, :, xh, z, part(c)],
            own_send.at[c, t], own_recv.at[c, s], (r, t),
        )

    def far_copy(c, t):
        return remote(
            sendbuf.at[t, 0, :, part(c)], weights.at[s, :, xh, z, part(c)],
            far_send.at[c, t], far_recv.at[c, s], (partner, t),
        )

    def update(c):
        rc = part(c)
        third[c].wait_recv()

        def step(b, _):
            gradient = z_sum(c, b, xh) + half_in[b, rc].astype(jnp.float32)
            new = adamw_update(master_ref[b, rc], one_ref[b, rc], two_ref[b, rc], gradient)
            for k in range(3):
                upd[k, b, rc] = new[k].astype(jnp.bfloat16)
            return 0

        lax.fori_loop(0, blocks, step, 0)

        def pack(t):
            for j in range(PAIR):
                index = chosen[t * PAIR + j]
                there = filled[t * PAIR + j] != 0
                for k in range(3):
                    value = upd[k, index, rc]
                    sendbuf[t, k, j, rc] = jnp.where(there, value, jnp.zeros_like(value))

        def deliver(i, _):
            t = lax.rem(s + i, sections)
            pack(t)
            own_copy(c, t).start()
            far_copy(c, t).start()
            mom_copy(c, t).start()
            return 0

        lax.fori_loop(1, sections, deliver, 0)
        pack(s)
        far_copy(c, s).start()
        for j in range(PAIR):
            weights[s, j, xh, z, rc] = sendbuf[s, 0, j, rc]
            moments[s, 0, j, rc] = sendbuf[s, 1, j, rc]
            moments[s, 1, j, rc] = sendbuf[s, 2, j, rc]

    def arrived(ref_of, sem_of, device):
        return remote(ref_of, ref_of, sem_of, sem_of, device)

    ring = [None] * PARTS

    def gather(c):
        rc = part(c)

        def take(i, _):
            t = lax.rem(s + i, sections)
            arrived(weights.at[t, :, xh, z, rc], own_recv.at[c, t], (r, t)).wait_recv()
            arrived(weights.at[t, :, 1 - xh, z, rc], far_recv.at[c, t], (partner, t)).wait_recv()
            return 0

        lax.fori_loop(1, sections, take, 0)
        arrived(weights.at[s, :, 1 - xh, z, rc], far_recv.at[c, s], (partner, s)).wait_recv()
        ring[c] = (
            remote(weights.at[:, :, 0, z, rc], weights.at[:, :, 0, z, rc], ring_send.at[c, 0], ring_recv.at[c, 0], dev_up),
            remote(weights.at[:, :, 1, z, rc], weights.at[:, :, 1, z, rc], ring_send.at[c, 1], ring_recv.at[c, 1], dev_down),
            remote(weights.at[:, :, 1, z, rc], weights.at[:, :, 1, z, rc], ring_send.at[c, 2], ring_recv.at[c, 2], dev_up),
            remote(weights.at[:, :, 0, z, rc], weights.at[:, :, 0, z, rc], ring_send.at[c, 3], ring_recv.at[c, 3], dev_down),
        )
        for copy in ring[c]:
            copy.start()

    onward = [None] * PARTS

    def forward(c):
        rc = part(c)
        onward[c] = (
            remote(weights.at[:, :, 0, down, rc], weights.at[:, :, 0, down, rc], fwd_send.at[c, 0], fwd_recv.at[c, 0], dev_up),
            remote(weights.at[:, :, 1, up, rc], weights.at[:, :, 1, up, rc], fwd_send.at[c, 1], fwd_recv.at[c, 1], dev_down),
        )
        arrived(weights.at[:, :, 0, down, rc], ring_recv.at[c, 0], dev_down).wait_recv()
        onward[c][0].start()
        arrived(weights.at[:, :, 1, up, rc], ring_recv.at[c, 1], dev_up).wait_recv()
        onward[c][1].start()

    def state(c):
        rc = part(c)

        def take(i, _):
            t = lax.rem(s + i, sections)
            arrived(moments.at[t, :, :, rc], mom_recv.at[c, t], (r, t)).wait_recv()
            return 0

        lax.fori_loop(1, sections, take, 0)

        def widen(t, _):
            for j in range(PAIR):
                out_master[t, j, rc] = weights[t, j, xh, z, rc].astype(jnp.float32)
                out_one[t, j, rc] = moments[t, 0, j, rc].astype(jnp.float32)
                out_two[t, j, rc] = moments[t, 1, j, rc].astype(jnp.float32)
            return 0

        lax.fori_loop(0, sections, widen, 0)

    stages = (join, cross, update, gather, forward, state)
    for tick in range(PARTS + len(stages) - 1):
        for number in reversed(range(len(stages))):
            c = tick - number
            if 0 <= c < PARTS:
                stages[number](c)

    for c in range(PARTS):
        rc = part(c)
        arrived(weights.at[:, :, 1, down, rc], ring_recv.at[c, 2], dev_down).wait_recv()
        arrived(weights.at[:, :, 0, up, rc], ring_recv.at[c, 3], dev_up).wait_recv()
        arrived(weights.at[:, :, 0, opposite, rc], fwd_recv.at[c, 0], dev_down).wait_recv()
        arrived(weights.at[:, :, 1, opposite, rc], fwd_recv.at[c, 1], dev_up).wait_recv()
        for copy in first[c] + second[c] + (third[c],) + ring[c] + onward[c]:
            copy.wait_send()

        def drain(i, _, c=c):
            t = lax.rem(s + i, sections)
            own_copy(c, t).wait_send()
            far_copy(c, t).wait_send()
            mom_copy(c, t).wait_send()
            return 0

        lax.fori_loop(1, sections, drain, 0)
        far_copy(c, s).wait_send()


def body(gradients, master, moment_one, moment_two, new_owner):
    sections = lax.axis_size("section")
    blocks, rows, lanes = master.shape
    bf16 = jnp.bfloat16
    f32 = jnp.float32
    grads = gradients.reshape(blocks, 2, 4, rows, lanes)
    owners = new_owner.reshape(1, -1)
    vmem = pl.BlockSpec(memory_space=pltpu.VMEM)
    state_shape = jax.ShapeDtypeStruct((sections, PAIR, rows, lanes), f32)
    dma = pltpu.SemaphoreType.DMA
    out = pl.pallas_call(
        functools.partial(kernel, sections),
        out_shape=(
            state_shape,
            state_shape,
            state_shape,
            jax.ShapeDtypeStruct((sections, PAIR, 2, 4, rows, lanes), bf16),
        ),
        in_specs=[
            pl.BlockSpec(memory_space=pltpu.SMEM),
            pl.BlockSpec(memory_space=pl.ANY),
            vmem,
            vmem,
            vmem,
        ],
        out_specs=(vmem, vmem, vmem, vmem),
        scratch_shapes=[
            pltpu.VMEM((blocks, 2, rows, lanes), bf16),
            pltpu.VMEM((2, blocks, rows, lanes), bf16),
            pltpu.VMEM((2, blocks, rows, lanes), bf16),
            pltpu.VMEM((2, blocks, rows, lanes), bf16),
            pltpu.VMEM((2, 2, blocks, rows, lanes), bf16),
            pltpu.VMEM((blocks, rows, lanes), bf16),
            pltpu.VMEM((blocks, rows, lanes), bf16),
            pltpu.VMEM((3, blocks, rows, lanes), bf16),
            pltpu.VMEM((sections, 3, PAIR, rows, lanes), bf16),
            pltpu.VMEM((sections, 2, PAIR, rows, lanes), bf16),
            pltpu.SMEM((sections * PAIR,), jnp.int32),
            pltpu.SMEM((sections * PAIR,), jnp.int32),
            dma((PARTS, 3)),
            dma((PARTS, 4)),
            dma((PARTS, 4)),
            dma((PARTS, 2)),
            dma((PARTS, 2)),
            dma((PARTS,)),
            dma((PARTS,)),
            dma((PARTS, sections)),
            dma((PARTS, sections)),
            dma((PARTS, sections)),
            dma((PARTS, sections)),
            dma((PARTS, sections)),
            dma((PARTS, sections)),
            dma((PARTS, 4)),
            dma((PARTS, 4)),
            dma((PARTS, 2)),
            dma((PARTS, 2)),
        ],
        compiler_params=pltpu.CompilerParams(
            collective_id=0, has_side_effects=True, vmem_limit_bytes=40 << 20
        ),
    )(owners, grads, master, moment_one, moment_two)
    weights = out[3].reshape(1, sections, PAIR, 8 * rows, lanes)
    return (out[0][None], out[1][None], out[2][None], weights)


def solution(mesh):
    placed = (
        P("replica", "section", None, None),
        P("section", "replica", None),
        P("section", "replica", None),
        P("section", "replica", None),
        P(),
    )
    return jax.shard_map(
        body,
        mesh=mesh,
        in_specs=placed,
        out_specs=(
            P("section", None, None, "replica", None),
            P("section", None, None, "replica", None),
            P("section", None, None, "replica", None),
            P("section", None, None, None, None),
        ),
        check_vma=False,
    )
```

```python
import functools

import jax
import jax.numpy as jnp
from jax import lax
from jax.experimental import pallas as pl
from jax.experimental.pallas import tpu as pltpu
from jax.sharding import PartitionSpec as P

MESH = pl.DeviceIdType.MESH
PAIR = 2
PARTS = 4
X_FIRST = (False, False, False, False)

beta_one = 0.9
beta_two = 0.95
step_count = 10.0
learn_rate = 0.01
decay_rate = 0.1
epsilon = 1e-08
correct_one = 1.0 - beta_one**step_count
correct_two = 1.0 - beta_two**step_count


def adamw_update(master, moment_one, moment_two, gradient):
    upd_one = beta_one * moment_one + (1.0 - beta_one) * gradient
    upd_two = beta_two * moment_two + (1.0 - beta_two) * gradient * gradient
    direction = upd_one / correct_one / (jnp.sqrt(upd_two / correct_two) + epsilon)
    upd_master = master - learn_rate * (direction + decay_rate * master)
    return (upd_master, upd_one, upd_two)


def kernel(
    sections,
    owner_hbm,
    grads_ref,
    master_hbm,
    one_hbm,
    two_hbm,
    out_master,
    out_one,
    out_two,
    weights,
    owner_ref,
    state_ref,
    own,
    near,
    half_out,
    half_in,
    upd,
    sendbuf,
    moments,
    chosen,
    filled,
    owner_sem,
    state_sem,
    load_sem,
    met_row,
    met_far,
    first_send,
    first_recv,
    half_send,
    half_recv,
    mom_send,
    mom_recv,
    own_send,
    own_recv,
    far_send,
    far_recv,
    ring_send,
    ring_recv,
    fwd_send,
    fwd_recv,
):
    blocks, rows = upd.shape[1], upd.shape[2]
    part_rows = rows // PARTS
    f32, bf16 = jnp.float32, jnp.bfloat16
    r = lax.axis_index("replica")
    s = lax.axis_index("section")
    xh = r // 4
    z = r % 4
    up = lax.rem(z + 1, 4)
    down = lax.rem(z + 3, 4)
    opposite = lax.rem(z + 2, 4)
    around = (up, down, opposite)
    dev_up = (xh * 4 + up, s)
    dev_down = (xh * 4 + down, s)
    dev_around = (dev_up, dev_down, (xh * 4 + opposite, s))
    partner = (1 - xh) * 4 + z

    def part(c):
        return pl.ds(c * part_rows, part_rows)

    def remote(src, dst, send, recv, device):
        return pltpu.make_async_remote_copy(
            src_ref=src, dst_ref=dst, send_sem=send, recv_sem=recv,
            device_id=device, device_id_type=MESH,
        )

    barrier = pltpu.get_barrier_semaphore()
    quad = [(s // 4) * 4 + lax.rem(s + i, 4) for i in range(1, 4)]
    row = [lax.rem(s + 4 * i, 16) for i in range(1, 4)]
    for device in dev_around + ((partner, s),):
        pl.semaphore_signal(barrier, inc=1, device_id=device, device_id_type=MESH)
    for t in quad + row:
        pl.semaphore_signal(barrier, inc=1, device_id=(r, t), device_id_type=MESH)

    owner_load = pltpu.make_async_copy(owner_hbm, owner_ref, owner_sem)
    owner_load.start()
    loads = []
    for c in range(PARTS):
        src = grads_ref.at[:, xh, :, part(c)] if X_FIRST[c] else grads_ref.at[:, :, z, part(c)]
        dst = own.at[:, :, part(c)] if X_FIRST[c] else own.at[:, pl.ds(0, 2), part(c)]
        loads.append(pltpu.make_async_copy(src, dst, load_sem.at[c]))
        loads[c].start()
    state_loads = []
    for k, src in enumerate((master_hbm, one_hbm, two_hbm)):
        state_loads.append(pltpu.make_async_copy(src, state_ref.at[k], state_sem.at[k]))
        state_loads[k].start()

    pl.semaphore_wait(barrier, 10)
    for t in row:
        pl.semaphore_signal(met_row, inc=1, device_id=(r, t), device_id_type=MESH)

    first = []
    for c in range(PARTS):
        rc = part(c)
        if X_FIRST[c]:
            first.append((
                remote(grads_ref.at[:, 1 - xh, :, rc], near.at[:, pl.ds(0, 4), rc], first_send.at[c, 0], first_recv.at[c, 0], (partner, s)),
            ))
        else:
            first.append(tuple(
                remote(grads_ref.at[:, :, around[k], rc], near.at[:, pl.ds(2 * k, 2), rc], first_send.at[c, k], first_recv.at[c, k], dev_around[k])
                for k in (2, 0, 1)
            ))
        for copy in first[c]:
            copy.start()

    owner_load.wait()
    for t in range(sections):
        one_at = jnp.int32(0)
        last_at = jnp.int32(0)
        count = jnp.int32(0)
        for i in reversed(range(blocks)):
            same = owner_ref[0, s * blocks + i] == t
            one_at = jnp.where(same, i, one_at)
            last_at = jnp.where(same & (count == 0), i, last_at)
            count = count + jnp.where(same, 1, 0)
        chosen[t * PAIR] = one_at
        chosen[t * PAIR + 1] = last_at
        filled[t * PAIR] = jnp.where(count > 0, 1, 0)
        filled[t * PAIR + 1] = jnp.where(count > 1, 1, 0)

    pl.semaphore_wait(met_row, 3)
    pl.semaphore_signal(met_far, inc=1, device_id=(partner, s), device_id_type=MESH)

    def first_sum(c, b, h):
        rc = part(c)
        total = own[b, h, rc].astype(f32)
        if X_FIRST[c]:
            return total + near[b, h, rc].astype(f32)
        for k in range(3):
            total = total + near[b, 2 * k + h, rc].astype(f32)
        return total

    second = [None] * PARTS

    def cross(c):
        rc = part(c)
        loads[c].wait()
        for copy in first[c]:
            copy.wait_recv()
        targets = tuple(zip(around, dev_around)) if X_FIRST[c] else ((1 - xh, (partner, s)),)
        second[c] = tuple(
            remote(half_out.at[k, :, rc], half_in.at[k, :, rc], half_send.at[c, k], half_recv.at[c, k], device)
            for k, (_, device) in enumerate(targets)
        )
        for k, (h, _) in enumerate(targets):

            def add(b, _, k=k, h=h):
                half_out[k, b, rc] = first_sum(c, b, h).astype(bf16)
                return 0

            lax.fori_loop(0, blocks, add, 0)
            second[c][k].start()

    def mom_copy(c, t):
        return remote(
            sendbuf.at[t, pl.ds(1, 2), :, part(c)], moments.at[s, :, :, part(c)],
            mom_send.at[c, t], mom_recv.at[c, s], (r, t),
        )

    def own_copy(c, t):
        return remote(
            sendbuf.at[t, 0, :, part(c)], weights.at[s, :, xh, z, part(c)],
            own_send.at[c, t], own_recv.at[c, s], (r, t),
        )

    def far_copy(c, t):
        return remote(
            sendbuf.at[t, 0, :, part(c)], weights.at[s, :, xh, z, part(c)],
            far_send.at[c, t], far_recv.at[c, s], (partner, t),
        )

    def update(c):
        rc = part(c)
        if c == 0:
            for copy in state_loads:
                copy.wait()
            pl.semaphore_wait(met_far, 1)
        for copy in second[c]:
            copy.wait_recv()

        def step(b, _):
            gradient = first_sum(c, b, z if X_FIRST[c] else xh)
            for k in range(len(second[c])):
                gradient = gradient + half_in[k, b, rc].astype(f32)
            new = adamw_update(state_ref[0, b, rc], state_ref[1, b, rc], state_ref[2, b, rc], gradient)
            for k in range(3):
                upd[k, b, rc] = new[k].astype(bf16)
            return 0

        lax.fori_loop(0, blocks, step, 0)

        def pack(t):
            for j in range(PAIR):
                index = chosen[t * PAIR + j]
                there = filled[t * PAIR + j] != 0
                for k in range(3):
                    value = upd[k, index, rc]
                    sendbuf[t, k, j, rc] = jnp.where(there, value, jnp.zeros_like(value))

        def deliver(i, _):
            t = lax.rem(s + i, sections)
            pack(t)
            own_copy(c, t).start()
            far_copy(c, t).start()
            mom_copy(c, t).start()
            return 0

        lax.fori_loop(1, sections, deliver, 0)
        pack(s)
        far_copy(c, s).start()
        for j in range(PAIR):
            weights[s, j, xh, z, rc] = sendbuf[s, 0, j, rc]
            moments[s, 0, j, rc] = sendbuf[s, 1, j, rc]
            moments[s, 1, j, rc] = sendbuf[s, 2, j, rc]

    def arrived(ref_of, sem_of, device):
        return remote(ref_of, ref_of, sem_of, sem_of, device)

    ring = [None] * PARTS

    def gather(c):
        rc = part(c)

        def take(i, _):
            t = lax.rem(s + i, sections)
            arrived(weights.at[t, :, xh, z, rc], own_recv.at[c, t], (r, t)).wait_recv()
            arrived(weights.at[t, :, 1 - xh, z, rc], far_recv.at[c, t], (partner, t)).wait_recv()
            return 0

        lax.fori_loop(1, sections, take, 0)
        arrived(weights.at[s, :, 1 - xh, z, rc], far_recv.at[c, s], (partner, s)).wait_recv()

        def along(h, k, device):
            ref = weights.at[:, :, h, z, rc]
            return remote(ref, ref, ring_send.at[c, k], ring_recv.at[c, k], device)

        ring[c] = (along(0, 0, dev_up), along(1, 1, dev_down), along(1, 2, dev_up), along(0, 3, dev_down))
        for copy in ring[c]:
            copy.start()

    onward = [None] * PARTS

    def forward(c):
        rc = part(c)
        from_down = weights.at[:, :, 0, down, rc]
        from_up = weights.at[:, :, 1, up, rc]
        onward[c] = (
            remote(from_down, from_down, fwd_send.at[c, 0], fwd_recv.at[c, 0], dev_up),
            remote(from_up, from_up, fwd_send.at[c, 1], fwd_recv.at[c, 1], dev_down),
        )
        arrived(from_down, ring_recv.at[c, 0], dev_down).wait_recv()
        onward[c][0].start()
        arrived(from_up, ring_recv.at[c, 1], dev_up).wait_recv()
        onward[c][1].start()

    def state(c):
        rc = part(c)

        def take(i, _):
            t = lax.rem(s + i, sections)
            arrived(moments.at[t, :, :, rc], mom_recv.at[c, t], (r, t)).wait_recv()
            return 0

        lax.fori_loop(1, sections, take, 0)

        def widen(t, _):
            for j in range(PAIR):
                out_master[t, j, rc] = weights[t, j, xh, z, rc].astype(f32)
                out_one[t, j, rc] = moments[t, 0, j, rc].astype(f32)
                out_two[t, j, rc] = moments[t, 1, j, rc].astype(f32)
            return 0

        lax.fori_loop(0, sections, widen, 0)

    stages = (cross, update, gather, forward, state)
    for tick in range(PARTS + len(stages) - 1):
        for number in reversed(range(len(stages))):
            c = tick - number
            if 0 <= c < PARTS:
                stages[number](c)

    for c in range(PARTS):
        rc = part(c)
        arrived(weights.at[:, :, 1, down, rc], ring_recv.at[c, 2], dev_down).wait_recv()
        arrived(weights.at[:, :, 0, up, rc], ring_recv.at[c, 3], dev_up).wait_recv()
        arrived(weights.at[:, :, 0, opposite, rc], fwd_recv.at[c, 0], dev_down).wait_recv()
        arrived(weights.at[:, :, 1, opposite, rc], fwd_recv.at[c, 1], dev_up).wait_recv()
        for copy in first[c] + second[c] + ring[c] + onward[c]:
            copy.wait_send()

        def drain(i, _, c=c):
            t = lax.rem(s + i, sections)
            own_copy(c, t).wait_send()
            far_copy(c, t).wait_send()
            mom_copy(c, t).wait_send()
            return 0

        lax.fori_loop(1, sections, drain, 0)
        far_copy(c, s).wait_send()


def store(*refs):
    count = len(refs) // 2
    sems = refs[-1]
    copies = [pltpu.make_async_copy(refs[k], refs[count + k], sems.at[k]) for k in range(count)]
    for copy in copies:
        copy.start()
    for copy in copies:
        copy.wait()


def body(gradients, master, moment_one, moment_two, new_owner):
    sections = lax.axis_size("section")
    blocks, rows, lanes = master.shape
    bf16 = jnp.bfloat16
    f32 = jnp.float32
    grads = gradients.reshape(blocks, 2, 4, rows, lanes)
    owners = new_owner.reshape(1, -1)
    vmem = pl.BlockSpec(memory_space=pltpu.VMEM)
    hbm = pl.BlockSpec(memory_space=pltpu.HBM)
    state_shape = jax.ShapeDtypeStruct((sections, PAIR, rows, lanes), f32)
    weight_shape = jax.ShapeDtypeStruct((sections, PAIR, 2, 4, rows, lanes), bf16)
    dma = pltpu.SemaphoreType.DMA
    regular = pltpu.SemaphoreType.REGULAR
    out = pl.pallas_call(
        functools.partial(kernel, sections),
        out_shape=(state_shape, state_shape, state_shape, weight_shape),
        in_specs=[hbm] * 5,
        out_specs=(vmem, vmem, vmem, vmem),
        scratch_shapes=[
            pltpu.SMEM(owners.shape, jnp.int32),
            pltpu.VMEM((3, blocks, rows, lanes), f32),
            pltpu.VMEM((blocks, 4, rows, lanes), bf16),
            pltpu.VMEM((blocks, 6, rows, lanes), bf16),
            pltpu.VMEM((3, blocks, rows, lanes), bf16),
            pltpu.VMEM((3, blocks, rows, lanes), bf16),
            pltpu.VMEM((3, blocks, rows, lanes), bf16),
            pltpu.VMEM((sections, 3, PAIR, rows, lanes), bf16),
            pltpu.VMEM((sections, 2, PAIR, rows, lanes), bf16),
            pltpu.SMEM((sections * PAIR,), jnp.int32),
            pltpu.SMEM((sections * PAIR,), jnp.int32),
            dma(()),
            dma((3,)),
            dma((PARTS,)),
            regular,
            regular,
            dma((PARTS, 3)),
            dma((PARTS, 3)),
            dma((PARTS, 3)),
            dma((PARTS, 3)),
            dma((PARTS, sections)),
            dma((PARTS, sections)),
            dma((PARTS, sections)),
            dma((PARTS, sections)),
            dma((PARTS, sections)),
            dma((PARTS, sections)),
            dma((PARTS, 4)),
            dma((PARTS, 4)),
            dma((PARTS, 2)),
            dma((PARTS, 2)),
        ],
        compiler_params=pltpu.CompilerParams(
            collective_id=0, has_side_effects=True, vmem_limit_bytes=40 << 20
        ),
    )(*[pltpu.with_memory_space_constraint(a, pltpu.HBM) for a in (owners, grads, master, moment_one, moment_two)])
    out = pl.pallas_call(
        store,
        out_shape=(state_shape, state_shape, state_shape, weight_shape),
        in_specs=[pl.BlockSpec(memory_space=pl.ANY)] * 4,
        out_specs=(hbm,) * 4,
        scratch_shapes=[dma((4,))],
        compiler_params=pltpu.CompilerParams(vmem_limit_bytes=1 << 20),
    )(*out)
    weights = out[3].reshape(1, sections, PAIR, 8 * rows, lanes)
    return (out[0][None], out[1][None], out[2][None], weights)


def solution(mesh):
    placed = (
        P("replica", "section", None, None),
        P("section", "replica", None),
        P("section", "replica", None),
        P("section", "replica", None),
        P(),
    )
    return jax.shard_map(
        body,
        mesh=mesh,
        in_specs=placed,
        out_specs=(
            P("section", None, None, "replica", None),
            P("section", None, None, "replica", None),
            P("section", None, None, "replica", None),
            P("section", None, None, None, None),
        ),
        check_vma=False,
    )
```

```python
import functools

import jax
import jax.numpy as jnp
from jax import lax
from jax.experimental import pallas as pl
from jax.experimental.pallas import tpu as pltpu
from jax.sharding import PartitionSpec as P

MESH = pl.DeviceIdType.MESH
PAIR = 2
PARTS = 4
DIRECT, JOIN, X_FIRST = range(3)
SUMS = (JOIN, JOIN, X_FIRST, JOIN)
Z_FIRST = (False, True, False, False)
ORDER = "j0 j1 x0 j2 x1 u0 j3 x2 u1 g0 x3 u2 g1 f0 u3 g2 f1 s0 g3 f2 l1 s1 f3 s2 s3"

beta_one = 0.9
beta_two = 0.95
step_count = 10.0
learn_rate = 0.01
decay_rate = 0.1
epsilon = 1e-08
correct_one = 1.0 - beta_one**step_count
correct_two = 1.0 - beta_two**step_count


def adamw_update(master, moment_one, moment_two, gradient):
    upd_one = beta_one * moment_one + (1.0 - beta_one) * gradient
    upd_two = beta_two * moment_two + (1.0 - beta_two) * gradient * gradient
    direction = upd_one / correct_one / (jnp.sqrt(upd_two / correct_two) + epsilon)
    upd_master = master - learn_rate * (direction + decay_rate * master)
    return (upd_master, upd_one, upd_two)


def kernel(
    sections,
    owner_hbm,
    grads_ref,
    master_hbm,
    one_hbm,
    two_hbm,
    out_master,
    out_one,
    out_two,
    weights,
    owner_ref,
    state_ref,
    own,
    near,
    mid_own,
    mid_out,
    half_out,
    half_in,
    upd,
    sendbuf,
    moments,
    chosen,
    filled,
    owner_sem,
    state_sem,
    load_sem,
    mid_sem,
    mid_send,
    mid_recv,
    met_row,
    met_far,
    first_send,
    first_recv,
    half_send,
    half_recv,
    mom_send,
    mom_recv,
    own_send,
    own_recv,
    far_send,
    far_recv,
    ring_send,
    ring_recv,
    fwd_send,
    fwd_recv,
    pass_send,
    pass_recv,
):
    blocks, rows = upd.shape[1], upd.shape[2]
    part_rows = rows // PARTS
    f32, bf16 = jnp.float32, jnp.bfloat16
    r = lax.axis_index("replica")
    s = lax.axis_index("section")
    xh = r // 4
    z = r % 4
    up = lax.rem(z + 1, 4)
    down = lax.rem(z + 3, 4)
    opposite = lax.rem(z + 2, 4)
    around = (up, down, opposite)
    dev_up = (xh * 4 + up, s)
    dev_down = (xh * 4 + down, s)
    dev_around = (dev_up, dev_down, (xh * 4 + opposite, s))
    partner = (1 - xh) * 4 + z

    def part(c):
        return pl.ds(c * part_rows, part_rows)

    def remote(src, dst, send, recv, device):
        return pltpu.make_async_remote_copy(
            src_ref=src, dst_ref=dst, send_sem=send, recv_sem=recv,
            device_id=device, device_id_type=MESH,
        )

    barrier = pltpu.get_barrier_semaphore()
    quad = [(s // 4) * 4 + lax.rem(s + i, 4) for i in range(1, 4)]
    row = [lax.rem(s + 4 * i, 16) for i in range(1, 4)]
    for device in dev_around + ((partner, s),):
        pl.semaphore_signal(barrier, inc=1, device_id=device, device_id_type=MESH)
    for t in quad + row:
        pl.semaphore_signal(barrier, inc=1, device_id=(r, t), device_id_type=MESH)

    owner_load = pltpu.make_async_copy(owner_hbm, owner_ref, owner_sem)
    owner_load.start()
    loads = []
    for c in range(PARTS):
        by_x = SUMS[c] == X_FIRST
        src = grads_ref.at[:, xh, :, part(c)] if by_x else grads_ref.at[:, :, z, part(c)]
        dst = own.at[:, :, part(c)] if by_x else own.at[:, pl.ds(0, 2), part(c)]
        loads.append(pltpu.make_async_copy(src, dst, load_sem.at[c]))
        loads[c].start()
    mid_loads = {}
    for c in range(PARTS):
        if SUMS[c] == JOIN:
            mid_loads[c] = (
                pltpu.make_async_copy(grads_ref.at[:, 0, up, part(c)], mid_own.at[0, :, part(c)], mid_sem.at[c, 0]),
                pltpu.make_async_copy(grads_ref.at[:, 1, down, part(c)], mid_own.at[1, :, part(c)], mid_sem.at[c, 1]),
            )
            for copy in mid_loads[c]:
                copy.start()
    state_loads = []
    for k, src in enumerate((master_hbm, one_hbm, two_hbm)):
        state_loads.append(pltpu.make_async_copy(src, state_ref.at[k], state_sem.at[k]))
        state_loads[k].start()

    pl.semaphore_wait(barrier, 10)
    for t in row:
        pl.semaphore_signal(met_row, inc=1, device_id=(r, t), device_id_type=MESH)

    first = []
    for c in range(PARTS):
        rc = part(c)
        if SUMS[c] == X_FIRST:
            first.append((
                remote(grads_ref.at[:, 1 - xh, :, rc], near.at[:, pl.ds(0, 4), rc], first_send.at[c, 0], first_recv.at[c, 0], (partner, s)),
            ))
        elif SUMS[c] == JOIN:
            first.append(tuple(
                remote(grads_ref.at[:, h, around[of], rc], near.at[:, slot, rc], first_send.at[c, k], first_recv.at[c, k], dev_around[to])
                for k, (h, of, to, slot) in enumerate(((0, 2, 0, 4), (1, 2, 1, 5), (1, 0, 0, 1), (0, 1, 1, 2)))
            ))
        else:
            first.append(tuple(
                remote(grads_ref.at[:, :, around[k], rc], near.at[:, pl.ds(2 * k, 2), rc], first_send.at[c, k], first_recv.at[c, k], dev_around[k])
                for k in (2, 0, 1)
            ))
        for copy in first[c]:
            copy.start()

    owner_load.wait()
    for t in range(sections):
        one_at = jnp.int32(0)
        last_at = jnp.int32(0)
        count = jnp.int32(0)
        for i in reversed(range(blocks)):
            same = owner_ref[0, s * blocks + i] == t
            one_at = jnp.where(same, i, one_at)
            last_at = jnp.where(same & (count == 0), i, last_at)
            count = count + jnp.where(same, 1, 0)
        chosen[t * PAIR] = one_at
        chosen[t * PAIR + 1] = last_at
        filled[t * PAIR] = jnp.where(count > 0, 1, 0)
        filled[t * PAIR + 1] = jnp.where(count > 1, 1, 0)

    pl.semaphore_wait(met_row, 3)
    pl.semaphore_signal(met_far, inc=1, device_id=(partner, s), device_id_type=MESH)

    def first_sum(c, b, h):
        rc = part(c)
        total = own[b, h, rc].astype(f32)
        if SUMS[c] == X_FIRST:
            return total + near[b, h, rc].astype(f32)
        for k in range(2 if SUMS[c] == JOIN else 3):
            total = total + near[b, 2 * k + h, rc].astype(f32)
        return total

    joined = [()] * PARTS

    def join(c):
        if SUMS[c] != JOIN:
            return
        rc = part(c)
        joined[c] = tuple(
            remote(mid_out.at[h, :, rc], near.at[:, 3 * h, rc], mid_send.at[c, h], mid_recv.at[c, h], dev_around[h])
            for h in range(2)
        )
        for h in range(2):
            mid_loads[c][h].wait()
            first[c][h].wait_recv()

            def add(b, _, h=h):
                mid_out[h, b, rc] = (near[b, 4 + h, rc].astype(f32) + mid_own[h, b, rc].astype(f32)).astype(bf16)
                return 0

            lax.fori_loop(0, blocks, add, 0)
            joined[c][h].start()

    second = [None] * PARTS

    def cross(c):
        rc = part(c)
        loads[c].wait()
        for copy in (first[c][2:] + joined[c]) if SUMS[c] == JOIN else first[c]:
            copy.wait_recv()
        targets = tuple(zip(around, dev_around)) if SUMS[c] == X_FIRST else ((1 - xh, (partner, s)),)
        second[c] = tuple(
            remote(half_out.at[k, :, rc], half_in.at[k, :, rc], half_send.at[c, k], half_recv.at[c, k], device)
            for k, (_, device) in enumerate(targets)
        )
        for k, (h, _) in enumerate(targets):

            def add(b, _, k=k, h=h):
                half_out[k, b, rc] = first_sum(c, b, h).astype(bf16)
                return 0

            lax.fori_loop(0, blocks, add, 0)
            second[c][k].start()

    def mom_copy(c, t):
        return remote(
            sendbuf.at[t, pl.ds(1, 2), :, part(c)], moments.at[s, :, :, part(c)],
            mom_send.at[c, t], mom_recv.at[c, s], (r, t),
        )

    def own_copy(c, t):
        return remote(
            sendbuf.at[t, 0, :, part(c)], weights.at[s, :, xh, z, part(c)],
            own_send.at[c, t], own_recv.at[c, s], (r, t),
        )

    def far_copy(c, t):
        return remote(
            sendbuf.at[t, 0, :, part(c)], weights.at[s, :, xh, z, part(c)],
            far_send.at[c, t], far_recv.at[c, s], (partner, t),
        )

    def update(c):
        rc = part(c)
        if c == 0:
            for copy in state_loads:
                copy.wait()
            pl.semaphore_wait(met_far, 1)
        for copy in second[c]:
            copy.wait_recv()

        def step(b, _):
            gradient = first_sum(c, b, z if SUMS[c] == X_FIRST else xh)
            for k in range(len(second[c])):
                gradient = gradient + half_in[k, b, rc].astype(f32)
            new = adamw_update(state_ref[0, b, rc], state_ref[1, b, rc], state_ref[2, b, rc], gradient)
            for k in range(3):
                upd[k, b, rc] = new[k].astype(bf16)
            return 0

        lax.fori_loop(0, blocks, step, 0)

        def pack(t):
            for j in range(PAIR):
                index = chosen[t * PAIR + j]
                there = filled[t * PAIR + j] != 0
                for k in range(3):
                    value = upd[k, index, rc]
                    sendbuf[t, k, j, rc] = jnp.where(there, value, jnp.zeros_like(value))

        def deliver(i, _):
            t = lax.rem(s + i, sections)
            pack(t)
            own_copy(c, t).start()
            if not Z_FIRST[c]:
                far_copy(c, t).start()
            mom_copy(c, t).start()
            return 0

        lax.fori_loop(1, sections, deliver, 0)
        pack(s)
        if not Z_FIRST[c]:
            far_copy(c, s).start()
        for j in range(PAIR):
            weights[s, j, xh, z, rc] = sendbuf[s, 0, j, rc]
            moments[s, 0, j, rc] = sendbuf[s, 1, j, rc]
            moments[s, 1, j, rc] = sendbuf[s, 2, j, rc]

    def arrived(ref_of, sem_of, device):
        return remote(ref_of, ref_of, sem_of, sem_of, device)

    ring = [None] * PARTS
    onward = [None] * PARTS
    passed = [()] * PARTS

    def shard(c, half, at):
        if Z_FIRST[c]:
            return weights.at[:, half, xh, at, part(c)]
        return weights.at[:, :, half, at, part(c)]

    def gather(c):
        rc = part(c)

        def take(i, _):
            t = lax.rem(s + i, sections)
            arrived(weights.at[t, :, xh, z, rc], own_recv.at[c, t], (r, t)).wait_recv()
            if not Z_FIRST[c]:
                arrived(weights.at[t, :, 1 - xh, z, rc], far_recv.at[c, t], (partner, t)).wait_recv()
            return 0

        lax.fori_loop(1, sections, take, 0)
        if not Z_FIRST[c]:
            arrived(weights.at[s, :, 1 - xh, z, rc], far_recv.at[c, s], (partner, s)).wait_recv()

        def along(half, k, device):
            ref = shard(c, half, z)
            return remote(ref, ref, ring_send.at[c, k], ring_recv.at[c, k], device)

        ring[c] = (along(0, 0, dev_up), along(1, 1, dev_down), along(1, 2, dev_up), along(0, 3, dev_down))
        for copy in ring[c]:
            copy.start()
        if Z_FIRST[c]:
            hand(c, weights.at[:, :, xh, z, rc], 0)

    def hand(c, ref, k):
        copy = remote(ref, ref, pass_send.at[c, k], pass_recv.at[c, k], (partner, s))
        copy.start()
        passed[c] += (copy,)

    def forward(c):
        from_down = shard(c, 0, down)
        from_up = shard(c, 1, up)
        onward[c] = (
            remote(from_down, from_down, fwd_send.at[c, 0], fwd_recv.at[c, 0], dev_up),
            remote(from_up, from_up, fwd_send.at[c, 1], fwd_recv.at[c, 1], dev_down),
        )
        arrived(from_down, ring_recv.at[c, 0], dev_down).wait_recv()
        onward[c][0].start()
        arrived(from_up, ring_recv.at[c, 1], dev_up).wait_recv()
        onward[c][1].start()
        if Z_FIRST[c]:
            rc = part(c)
            arrived(shard(c, 1, down), ring_recv.at[c, 2], dev_down).wait_recv()
            hand(c, weights.at[:, :, xh, down, rc], 1)
            arrived(shard(c, 0, up), ring_recv.at[c, 3], dev_up).wait_recv()
            hand(c, weights.at[:, :, xh, up, rc], 2)

    def last(c):
        rc = part(c)
        arrived(shard(c, 0, opposite), fwd_recv.at[c, 0], dev_down).wait_recv()
        arrived(shard(c, 1, opposite), fwd_recv.at[c, 1], dev_up).wait_recv()
        if Z_FIRST[c]:
            hand(c, weights.at[:, :, xh, opposite, rc], 3)

    def state(c):
        rc = part(c)

        def take(i, _):
            t = lax.rem(s + i, sections)
            arrived(moments.at[t, :, :, rc], mom_recv.at[c, t], (r, t)).wait_recv()
            return 0

        lax.fori_loop(1, sections, take, 0)

        def widen(t, _):
            for j in range(PAIR):
                out_master[t, j, rc] = weights[t, j, xh, z, rc].astype(f32)
                out_one[t, j, rc] = moments[t, 0, j, rc].astype(f32)
                out_two[t, j, rc] = moments[t, 1, j, rc].astype(f32)
            return 0

        lax.fori_loop(0, sections, widen, 0)

    stages = dict(j=join, x=cross, u=update, g=gather, f=forward, l=last, s=state)
    for step in ORDER.split():
        stages[step[0]](int(step[1]))

    for c in range(PARTS):
        if not Z_FIRST[c]:
            last(c)
            arrived(shard(c, 1, down), ring_recv.at[c, 2], dev_down).wait_recv()
            arrived(shard(c, 0, up), ring_recv.at[c, 3], dev_up).wait_recv()
        else:
            for k, at in enumerate((z, down, up, opposite)):
                arrived(weights.at[:, :, 1 - xh, at, part(c)], pass_recv.at[c, k], (partner, s)).wait_recv()
        for copy in first[c] + joined[c] + second[c] + ring[c] + onward[c] + passed[c]:
            copy.wait_send()

        def drain(i, _, c=c):
            t = lax.rem(s + i, sections)
            own_copy(c, t).wait_send()
            if not Z_FIRST[c]:
                far_copy(c, t).wait_send()
            mom_copy(c, t).wait_send()
            return 0

        lax.fori_loop(1, sections, drain, 0)
        if not Z_FIRST[c]:
            far_copy(c, s).wait_send()


def store(*refs):
    count = len(refs) // 2
    sems = refs[-1]
    copies = [pltpu.make_async_copy(refs[k], refs[count + k], sems.at[k]) for k in range(count)]
    for copy in copies:
        copy.start()
    for copy in copies:
        copy.wait()


def body(gradients, master, moment_one, moment_two, new_owner):
    sections = lax.axis_size("section")
    blocks, rows, lanes = master.shape
    bf16 = jnp.bfloat16
    f32 = jnp.float32
    grads = gradients.reshape(blocks, 2, 4, rows, lanes)
    owners = new_owner.reshape(1, -1)
    vmem = pl.BlockSpec(memory_space=pltpu.VMEM)
    hbm = pl.BlockSpec(memory_space=pltpu.HBM)
    state_shape = jax.ShapeDtypeStruct((sections, PAIR, rows, lanes), f32)
    weight_shape = jax.ShapeDtypeStruct((sections, PAIR, 2, 4, rows, lanes), bf16)
    dma = pltpu.SemaphoreType.DMA
    regular = pltpu.SemaphoreType.REGULAR
    out = pl.pallas_call(
        functools.partial(kernel, sections),
        out_shape=(state_shape, state_shape, state_shape, weight_shape),
        in_specs=[hbm] * 5,
        out_specs=(vmem, vmem, vmem, vmem),
        scratch_shapes=[
            pltpu.SMEM(owners.shape, jnp.int32),
            pltpu.VMEM((3, blocks, rows, lanes), f32),
            pltpu.VMEM((blocks, 4, rows, lanes), bf16),
            pltpu.VMEM((blocks, 6, rows, lanes), bf16),
            pltpu.VMEM((2, blocks, rows, lanes), bf16),
            pltpu.VMEM((2, blocks, rows, lanes), bf16),
            pltpu.VMEM((3, blocks, rows, lanes), bf16),
            pltpu.VMEM((3, blocks, rows, lanes), bf16),
            pltpu.VMEM((3, blocks, rows, lanes), bf16),
            pltpu.VMEM((sections, 3, PAIR, rows, lanes), bf16),
            pltpu.VMEM((sections, 2, PAIR, rows, lanes), bf16),
            pltpu.SMEM((sections * PAIR,), jnp.int32),
            pltpu.SMEM((sections * PAIR,), jnp.int32),
            dma(()),
            dma((3,)),
            dma((PARTS,)),
            dma((PARTS, 2)),
            dma((PARTS, 2)),
            dma((PARTS, 2)),
            regular,
            regular,
            dma((PARTS, 4)),
            dma((PARTS, 4)),
            dma((PARTS, 3)),
            dma((PARTS, 3)),
            dma((PARTS, sections)),
            dma((PARTS, sections)),
            dma((PARTS, sections)),
            dma((PARTS, sections)),
            dma((PARTS, sections)),
            dma((PARTS, sections)),
            dma((PARTS, 4)),
            dma((PARTS, 4)),
            dma((PARTS, 2)),
            dma((PARTS, 2)),
            dma((PARTS, 4)),
            dma((PARTS, 4)),
        ],
        compiler_params=pltpu.CompilerParams(
            collective_id=0, has_side_effects=True, vmem_limit_bytes=40 << 20
        ),
    )(*[pltpu.with_memory_space_constraint(a, pltpu.HBM) for a in (owners, grads, master, moment_one, moment_two)])
    out = pl.pallas_call(
        store,
        out_shape=(state_shape, state_shape, state_shape, weight_shape),
        in_specs=[pl.BlockSpec(memory_space=pl.ANY)] * 4,
        out_specs=(hbm,) * 4,
        scratch_shapes=[dma((4,))],
        compiler_params=pltpu.CompilerParams(vmem_limit_bytes=1 << 20),
    )(*out)
    weights = out[3].reshape(1, sections, PAIR, 8 * rows, lanes)
    return (out[0][None], out[1][None], out[2][None], weights)


def solution(mesh):
    placed = (
        P("replica", "section", None, None),
        P("section", "replica", None),
        P("section", "replica", None),
        P("section", "replica", None),
        P(),
    )
    return jax.shard_map(
        body,
        mesh=mesh,
        in_specs=placed,
        out_specs=(
            P("section", None, None, "replica", None),
            P("section", None, None, "replica", None),
            P("section", None, None, "replica", None),
            P("section", None, None, None, None),
        ),
        check_vma=False,
    )
```

```python
import functools

import jax
import jax.numpy as jnp
from jax import lax
from jax.experimental import pallas as pl
from jax.experimental.pallas import tpu as pltpu
from jax.sharding import PartitionSpec as P

MESH = pl.DeviceIdType.MESH
PAIR = 2
PARTS = 4
DIRECT, JOIN, X_FIRST = range(3)
SUMS = (JOIN, JOIN, X_FIRST, JOIN)
Z_FIRST = (False, True, False, False)
ORDER = (
    ("j", 0), ("j", 1), ("x", 0), ("j", 2), ("x", 1), ("u", 0),
    ("j", 3), ("x", 2), ("u", 1), ("g", 0), ("x", 3), ("u", 2),
    ("g", 1), ("f", 0), ("u", 3), ("g", 2), ("f", 1), ("g", 3),
    ("f", 2), ("l", 1), ("f", 3), ("s", 0), ("s", 1), ("s", 2),
    ("s", 3),
)

beta_one = 0.9
beta_two = 0.95
step_count = 10.0
learn_rate = 0.01
decay_rate = 0.1
epsilon = 1e-08
correct_one = 1.0 - beta_one**step_count
correct_two = 1.0 - beta_two**step_count


def adamw_update(master, moment_one, moment_two, gradient):
    upd_one = beta_one * moment_one + (1.0 - beta_one) * gradient
    upd_two = beta_two * moment_two + (1.0 - beta_two) * gradient * gradient
    direction = upd_one / correct_one / (jnp.sqrt(upd_two / correct_two) + epsilon)
    upd_master = master - learn_rate * (direction + decay_rate * master)
    return (upd_master, upd_one, upd_two)


def kernel(
    sections,
    owner_hbm,
    grads_ref,
    master_hbm,
    one_hbm,
    two_hbm,
    out_master,
    out_one,
    out_two,
    weights,
    owner_ref,
    state_ref,
    own,
    near,
    mid_own,
    mid_out,
    half_out,
    half_in,
    upd,
    sendbuf,
    moments,
    chosen,
    filled,
    owner_sem,
    state_sem,
    load_sem,
    mid_sem,
    mid_send,
    mid_recv,
    met_row,
    met_far,
    first_send,
    first_recv,
    half_send,
    half_recv,
    mom_send,
    mom_recv,
    own_send,
    own_recv,
    far_send,
    far_recv,
    ring_send,
    ring_recv,
    fwd_send,
    fwd_recv,
    pass_send,
    pass_recv,
):
    blocks, rows = upd.shape[1], upd.shape[2]
    part_rows = rows // PARTS
    f32, bf16 = jnp.float32, jnp.bfloat16
    r = lax.axis_index("replica")
    s = lax.axis_index("section")
    xh = r // 4
    z = r % 4
    up = lax.rem(z + 1, 4)
    down = lax.rem(z + 3, 4)
    opposite = lax.rem(z + 2, 4)
    around = (up, down, opposite)
    dev_up = (xh * 4 + up, s)
    dev_down = (xh * 4 + down, s)
    dev_around = (dev_up, dev_down, (xh * 4 + opposite, s))
    partner = (1 - xh) * 4 + z

    def part(c):
        return pl.ds(c * part_rows, part_rows)

    def remote(src, dst, send, recv, device):
        return pltpu.make_async_remote_copy(
            src_ref=src, dst_ref=dst, send_sem=send, recv_sem=recv,
            device_id=device, device_id_type=MESH,
        )

    barrier = pltpu.get_barrier_semaphore()
    quad = [(s // 4) * 4 + lax.rem(s + i, 4) for i in range(1, 4)]
    row = [lax.rem(s + 4 * i, 16) for i in range(1, 4)]
    for device in dev_around + ((partner, s),):
        pl.semaphore_signal(barrier, inc=1, device_id=device, device_id_type=MESH)
    for t in quad + row:
        pl.semaphore_signal(barrier, inc=1, device_id=(r, t), device_id_type=MESH)

    owner_load = pltpu.make_async_copy(owner_hbm, owner_ref, owner_sem)
    owner_load.start()
    loads = []
    for c in range(PARTS):
        by_x = SUMS[c] == X_FIRST
        src = grads_ref.at[:, xh, :, part(c)] if by_x else grads_ref.at[:, :, z, part(c)]
        dst = own.at[:, :, part(c)] if by_x else own.at[:, pl.ds(0, 2), part(c)]
        loads.append(pltpu.make_async_copy(src, dst, load_sem.at[c]))
        loads[c].start()
    mid_loads = {}
    for c in range(PARTS):
        if SUMS[c] == JOIN:
            mid_loads[c] = (
                pltpu.make_async_copy(grads_ref.at[:, 0, up, part(c)], mid_own.at[0, :, part(c)], mid_sem.at[c, 0]),
                pltpu.make_async_copy(grads_ref.at[:, 1, down, part(c)], mid_own.at[1, :, part(c)], mid_sem.at[c, 1]),
            )
            for copy in mid_loads[c]:
                copy.start()
    state_loads = []
    for k, src in enumerate((master_hbm, one_hbm, two_hbm)):
        state_loads.append(pltpu.make_async_copy(src, state_ref.at[k], state_sem.at[k]))
        state_loads[k].start()

    pl.semaphore_wait(barrier, 10)
    for t in row:
        pl.semaphore_signal(met_row, inc=1, device_id=(r, t), device_id_type=MESH)

    first = []
    for c in range(PARTS):
        rc = part(c)
        if SUMS[c] == X_FIRST:
            first.append((
                remote(grads_ref.at[:, 1 - xh, :, rc], near.at[:, pl.ds(0, 4), rc], first_send.at[c, 0], first_recv.at[c, 0], (partner, s)),
            ))
        elif SUMS[c] == JOIN:
            first.append(tuple(
                remote(grads_ref.at[:, h, around[of], rc], near.at[:, slot, rc], first_send.at[c, k], first_recv.at[c, k], dev_around[to])
                for k, (h, of, to, slot) in enumerate(((0, 2, 0, 4), (1, 2, 1, 5), (1, 0, 0, 1), (0, 1, 1, 2)))
            ))
        else:
            first.append(tuple(
                remote(grads_ref.at[:, :, around[k], rc], near.at[:, pl.ds(2 * k, 2), rc], first_send.at[c, k], first_recv.at[c, k], dev_around[k])
                for k in (2, 0, 1)
            ))
        for copy in first[c]:
            copy.start()

    owner_load.wait()
    for t in range(sections):
        one_at = jnp.int32(0)
        last_at = jnp.int32(0)
        count = jnp.int32(0)
        for i in reversed(range(blocks)):
            same = owner_ref[0, s * blocks + i] == t
            one_at = jnp.where(same, i, one_at)
            last_at = jnp.where(same & (count == 0), i, last_at)
            count = count + jnp.where(same, 1, 0)
        chosen[t * PAIR] = one_at
        chosen[t * PAIR + 1] = last_at
        filled[t * PAIR] = jnp.where(count > 0, 1, 0)
        filled[t * PAIR + 1] = jnp.where(count > 1, 1, 0)

    pl.semaphore_wait(met_row, 3)
    pl.semaphore_signal(met_far, inc=1, device_id=(partner, s), device_id_type=MESH)

    def first_sum(c, b, h):
        rc = part(c)
        total = own[b, h, rc].astype(f32)
        if SUMS[c] == X_FIRST:
            return total + near[b, h, rc].astype(f32)
        for k in range(2 if SUMS[c] == JOIN else 3):
            total = total + near[b, 2 * k + h, rc].astype(f32)
        return total

    joined = [()] * PARTS

    def join(c):
        if SUMS[c] != JOIN:
            return
        rc = part(c)
        joined[c] = tuple(
            remote(mid_out.at[h, :, rc], near.at[:, 3 * h, rc], mid_send.at[c, h], mid_recv.at[c, h], dev_around[h])
            for h in range(2)
        )
        for h in range(2):
            mid_loads[c][h].wait()
            first[c][h].wait_recv()

            def add(b, _, h=h):
                mid_out[h, b, rc] = (near[b, 4 + h, rc].astype(f32) + mid_own[h, b, rc].astype(f32)).astype(bf16)
                return 0

            lax.fori_loop(0, blocks, add, 0)
            joined[c][h].start()

    second = [None] * PARTS

    def cross(c):
        rc = part(c)
        loads[c].wait()
        for copy in (first[c][2:] + joined[c]) if SUMS[c] == JOIN else first[c]:
            copy.wait_recv()
        targets = tuple(zip(around, dev_around)) if SUMS[c] == X_FIRST else ((1 - xh, (partner, s)),)
        second[c] = tuple(
            remote(half_out.at[k, :, rc], half_in.at[k, :, rc], half_send.at[c, k], half_recv.at[c, k], device)
            for k, (_, device) in enumerate(targets)
        )
        for k, (h, _) in enumerate(targets):

            def add(b, _, k=k, h=h):
                half_out[k, b, rc] = first_sum(c, b, h).astype(bf16)
                return 0

            lax.fori_loop(0, blocks, add, 0)
            second[c][k].start()

    def mom_copy(c, t):
        return remote(
            sendbuf.at[t, pl.ds(1, 2), :, part(c)], moments.at[s, :, :, part(c)],
            mom_send.at[c, t], mom_recv.at[c, s], (r, t),
        )

    def own_copy(c, t):
        return remote(
            sendbuf.at[t, 0, :, part(c)], weights.at[s, :, xh, z, part(c)],
            own_send.at[c, t], own_recv.at[c, s], (r, t),
        )

    def far_copy(c, t):
        return remote(
            sendbuf.at[t, 0, :, part(c)], weights.at[s, :, xh, z, part(c)],
            far_send.at[c, t], far_recv.at[c, s], (partner, t),
        )

    def update(c):
        rc = part(c)
        if c == 0:
            for copy in state_loads:
                copy.wait()
            pl.semaphore_wait(met_far, 1)
        for copy in second[c]:
            copy.wait_recv()

        def step(b, _):
            gradient = first_sum(c, b, z if SUMS[c] == X_FIRST else xh)
            for k in range(len(second[c])):
                gradient = gradient + half_in[k, b, rc].astype(f32)
            new = adamw_update(state_ref[0, b, rc], state_ref[1, b, rc], state_ref[2, b, rc], gradient)
            for k in range(3):
                upd[k, b, rc] = new[k].astype(bf16)
            return 0

        lax.fori_loop(0, blocks, step, 0)

        def pack(t):
            for j in range(PAIR):
                index = chosen[t * PAIR + j]
                there = filled[t * PAIR + j] != 0
                for k in range(3):
                    value = upd[k, index, rc]
                    sendbuf[t, k, j, rc] = jnp.where(there, value, jnp.zeros_like(value))

        def deliver(i, _):
            t = lax.rem(s + i, sections)
            pack(t)
            own_copy(c, t).start()
            if not Z_FIRST[c]:
                far_copy(c, t).start()
            mom_copy(c, t).start()
            return 0

        lax.fori_loop(1, sections, deliver, 0)
        pack(s)
        if not Z_FIRST[c]:
            far_copy(c, s).start()
        for j in range(PAIR):
            weights[s, j, xh, z, rc] = sendbuf[s, 0, j, rc]
            moments[s, 0, j, rc] = sendbuf[s, 1, j, rc]
            moments[s, 1, j, rc] = sendbuf[s, 2, j, rc]

    def arrived(ref_of, sem_of, device):
        return remote(ref_of, ref_of, sem_of, sem_of, device)

    ring = [None] * PARTS
    onward = [None] * PARTS
    passed = [()] * PARTS

    def shard(c, half, at):
        if Z_FIRST[c]:
            return weights.at[:, half, xh, at, part(c)]
        return weights.at[:, :, half, at, part(c)]

    def gather(c):
        rc = part(c)

        def take(i, _):
            t = lax.rem(s + i, sections)
            arrived(weights.at[t, :, xh, z, rc], own_recv.at[c, t], (r, t)).wait_recv()
            if not Z_FIRST[c]:
                arrived(weights.at[t, :, 1 - xh, z, rc], far_recv.at[c, t], (partner, t)).wait_recv()
            return 0

        lax.fori_loop(1, sections, take, 0)
        if not Z_FIRST[c]:
            arrived(weights.at[s, :, 1 - xh, z, rc], far_recv.at[c, s], (partner, s)).wait_recv()

        def along(half, k, device):
            ref = shard(c, half, z)
            return remote(ref, ref, ring_send.at[c, k], ring_recv.at[c, k], device)

        ring[c] = (along(0, 0, dev_up), along(1, 1, dev_down), along(1, 2, dev_up), along(0, 3, dev_down))
        for copy in ring[c]:
            copy.start()
        if Z_FIRST[c]:
            hand(c, weights.at[:, :, xh, z, rc], 0)

    def hand(c, ref, k):
        copy = remote(ref, ref, pass_send.at[c, k], pass_recv.at[c, k], (partner, s))
        copy.start()
        passed[c] += (copy,)

    def forward(c):
        from_down = shard(c, 0, down)
        from_up = shard(c, 1, up)
        onward[c] = (
            remote(from_down, from_down, fwd_send.at[c, 0], fwd_recv.at[c, 0], dev_up),
            remote(from_up, from_up, fwd_send.at[c, 1], fwd_recv.at[c, 1], dev_down),
        )
        arrived(from_down, ring_recv.at[c, 0], dev_down).wait_recv()
        onward[c][0].start()
        arrived(from_up, ring_recv.at[c, 1], dev_up).wait_recv()
        onward[c][1].start()
        if Z_FIRST[c]:
            rc = part(c)
            arrived(shard(c, 1, down), ring_recv.at[c, 2], dev_down).wait_recv()
            hand(c, weights.at[:, :, xh, down, rc], 1)
            arrived(shard(c, 0, up), ring_recv.at[c, 3], dev_up).wait_recv()
            hand(c, weights.at[:, :, xh, up, rc], 2)

    def last(c):
        rc = part(c)
        arrived(shard(c, 0, opposite), fwd_recv.at[c, 0], dev_down).wait_recv()
        arrived(shard(c, 1, opposite), fwd_recv.at[c, 1], dev_up).wait_recv()
        if Z_FIRST[c]:
            hand(c, weights.at[:, :, xh, opposite, rc], 3)

    def state(c):
        rc = part(c)

        def take(i, _):
            t = lax.rem(s + i, sections)
            arrived(moments.at[t, :, :, rc], mom_recv.at[c, t], (r, t)).wait_recv()
            return 0

        lax.fori_loop(1, sections, take, 0)

        def widen(t, _):
            for j in range(PAIR):
                out_master[t, j, rc] = weights[t, j, xh, z, rc].astype(f32)
                out_one[t, j, rc] = moments[t, 0, j, rc].astype(f32)
                out_two[t, j, rc] = moments[t, 1, j, rc].astype(f32)
            return 0

        lax.fori_loop(0, sections, widen, 0)

    stages = dict(j=join, x=cross, u=update, g=gather, f=forward, l=last, s=state)
    for name, c in ORDER:
        stages[name](c)

    for c in range(PARTS):
        if not Z_FIRST[c]:
            last(c)
            arrived(shard(c, 1, down), ring_recv.at[c, 2], dev_down).wait_recv()
            arrived(shard(c, 0, up), ring_recv.at[c, 3], dev_up).wait_recv()
        else:
            for k, at in enumerate((z, down, up, opposite)):
                arrived(weights.at[:, :, 1 - xh, at, part(c)], pass_recv.at[c, k], (partner, s)).wait_recv()
        for copy in first[c] + joined[c] + second[c] + ring[c] + onward[c] + passed[c]:
            copy.wait_send()

        def drain(i, _, c=c):
            t = lax.rem(s + i, sections)
            own_copy(c, t).wait_send()
            if not Z_FIRST[c]:
                far_copy(c, t).wait_send()
            mom_copy(c, t).wait_send()
            return 0

        lax.fori_loop(1, sections, drain, 0)
        if not Z_FIRST[c]:
            far_copy(c, s).wait_send()


def store(*refs):
    count = len(refs) // 2
    sems = refs[-1]
    copies = [pltpu.make_async_copy(refs[k], refs[count + k], sems.at[k]) for k in range(count)]
    for copy in copies:
        copy.start()
    for copy in copies:
        copy.wait()


def body(gradients, master, moment_one, moment_two, new_owner):
    sections = lax.axis_size("section")
    blocks, rows, lanes = master.shape
    bf16 = jnp.bfloat16
    f32 = jnp.float32
    grads = gradients.reshape(blocks, 2, 4, rows, lanes)
    owners = new_owner.reshape(1, -1)
    vmem = pl.BlockSpec(memory_space=pltpu.VMEM)
    hbm = pl.BlockSpec(memory_space=pltpu.HBM)
    state_shape = jax.ShapeDtypeStruct((sections, PAIR, rows, lanes), f32)
    weight_shape = jax.ShapeDtypeStruct((sections, PAIR, 2, 4, rows, lanes), bf16)
    dma = pltpu.SemaphoreType.DMA
    regular = pltpu.SemaphoreType.REGULAR
    out = pl.pallas_call(
        functools.partial(kernel, sections),
        out_shape=(state_shape, state_shape, state_shape, weight_shape),
        in_specs=[hbm] * 5,
        out_specs=(vmem, vmem, vmem, vmem),
        scratch_shapes=[
            pltpu.SMEM(owners.shape, jnp.int32),
            pltpu.VMEM((3, blocks, rows, lanes), f32),
            pltpu.VMEM((blocks, 4, rows, lanes), bf16),
            pltpu.VMEM((blocks, 6, rows, lanes), bf16),
            pltpu.VMEM((2, blocks, rows, lanes), bf16),
            pltpu.VMEM((2, blocks, rows, lanes), bf16),
            pltpu.VMEM((3, blocks, rows, lanes), bf16),
            pltpu.VMEM((3, blocks, rows, lanes), bf16),
            pltpu.VMEM((3, blocks, rows, lanes), bf16),
            pltpu.VMEM((sections, 3, PAIR, rows, lanes), bf16),
            pltpu.VMEM((sections, 2, PAIR, rows, lanes), bf16),
            pltpu.SMEM((sections * PAIR,), jnp.int32),
            pltpu.SMEM((sections * PAIR,), jnp.int32),
            dma(()),
            dma((3,)),
            dma((PARTS,)),
            dma((PARTS, 2)),
            dma((PARTS, 2)),
            dma((PARTS, 2)),
            regular,
            regular,
            dma((PARTS, 4)),
            dma((PARTS, 4)),
            dma((PARTS, 3)),
            dma((PARTS, 3)),
            dma((PARTS, sections)),
            dma((PARTS, sections)),
            dma((PARTS, sections)),
            dma((PARTS, sections)),
            dma((PARTS, sections)),
            dma((PARTS, sections)),
            dma((PARTS, 4)),
            dma((PARTS, 4)),
            dma((PARTS, 2)),
            dma((PARTS, 2)),
            dma((PARTS, 4)),
            dma((PARTS, 4)),
        ],
        compiler_params=pltpu.CompilerParams(
            collective_id=0, has_side_effects=True, vmem_limit_bytes=40 << 20
        ),
    )(*[pltpu.with_memory_space_constraint(a, pltpu.HBM) for a in (owners, grads, master, moment_one, moment_two)])
    out = pl.pallas_call(
        store,
        out_shape=(state_shape, state_shape, state_shape, weight_shape),
        in_specs=[pl.BlockSpec(memory_space=pl.ANY)] * 4,
        out_specs=(hbm,) * 4,
        scratch_shapes=[dma((4,))],
        compiler_params=pltpu.CompilerParams(vmem_limit_bytes=1 << 20),
    )(*out)
    weights = out[3].reshape(1, sections, PAIR, 8 * rows, lanes)
    return (out[0][None], out[1][None], out[2][None], weights)


def solution(mesh):
    placed = (
        P("replica", "section", None, None),
        P("section", "replica", None),
        P("section", "replica", None),
        P("section", "replica", None),
        P(),
    )
    return jax.shard_map(
        body,
        mesh=mesh,
        in_specs=placed,
        out_specs=(
            P("section", None, None, "replica", None),
            P("section", None, None, "replica", None),
            P("section", None, None, "replica", None),
            P("section", None, None, None, None),
        ),
        check_vma=False,
    )
```
